256 devices in a mesh: prow: 16 (over z_lo, y, core), pcol: 16 (over z_hi, x).
Axes of the slice: x: 4, y: 4, z: 8 (z_hi: 4, z_lo: 2; z = z_hi * 2 + z_lo), core: 2. Of those that a mesh axis runs over, the one named last changes fastest.
Arguments:
- rhs_panel: float32 [2, 768, 2048], P(None, None, 'pcol'), may hold values from -6 to 6
- diag_inverse: float32 [2, 2048, 2048], P(None, 'prow', 'pcol'), may hold values from -0.125 to 0.125
- sub_block: float32 [2048, 2048], P('pcol', 'prow'), may hold values from -0.125 to 0.125
- lower_panels: float32 [98304, 4096], P(('prow', 'pcol')), may hold values from -0.09375 to 0.09375
- rhs_tail: float32 [768, 98304], P(None, ('prow', 'pcol')), may hold values from -6 to 6
- solved_tail: float32 [768, 98304], P(None, ('prow', 'pcol')), may hold values from -1.2 to 1.2
Outputs:
- rhs_updated: float32 [768, 98304], P(None, ('prow', 'pcol'))
- solved_panel: float32 [2, 768, 2048], P(None, None, 'pcol')
The draws below stay inside these ranges and needn't reach their ends.
All inputs are finite; a program needn't handle non-finite values.
Results may differ from the reference program's by a relative error of at most 0.000073.
Values sent between devices are 32-bit elements; how exact they have to be, the bound alone decides.
No kernel may reach another device: no remote copies, remote signals or barrier semaphores. Data moves between devices by JAX's collectives and lax.ppermute only.
A program may use at most 128 MiB of HBM per device.

```python
import jax
import jax.numpy as jnp
from jax import lax

W = 2048
M = 768
TAIL = 98304


def block_levels(rng, shape, cuts, smallest, top_value):
    level = 1.0
    for axis_at, blocks in cuts:
        draws = jax.random.uniform(jax.random.fold_in(jax.random.fold_in(rng, 6), axis_at), (blocks,), jnp.float32, smallest / len(cuts), top_value / len(cuts))
        level = level * jnp.repeat(jnp.exp(draws), shape[axis_at] // blocks).reshape((-1,) + (1,) * (len(shape) - 1 - axis_at))
    return level


def bell_draw(key, dims, deviation, most, split=(), kind=jnp.bfloat16):
    result = jax.random.normal(key, dims, jnp.float32) * deviation
    if len(split) > 0:
        result = block_levels(key, dims, split, -0.22, 0.18) * result
    return jnp.clip(result, min=-most, max=most).astype(kind)


def setup_inputs(seed: int = 0) -> dict:
    keys = jax.random.split(jax.random.key(seed), 7)
    return {
        "rhs_panel": bell_draw(keys[0], (2, M, W), 1.0, 6.0, ((2, 16),), jnp.float32),
        "diag_inverse": bell_draw(keys[1], (2, W, W), W ** -0.5, 0.125, ((1, 16), (2, 16)), jnp.float32),
        "sub_block": bell_draw(keys[2], (W, W), W ** -0.5, 0.125, ((0, 16), (1, 16)), jnp.float32),
        "lower_panels": bell_draw(keys[3], (TAIL, 2 * W), (2 * W) ** -0.5, 0.09375, ((0, 256),), jnp.float32),
        "rhs_tail": bell_draw(keys[4], (M, TAIL), 1.0, 6.0, ((1, 256),), jnp.float32),
        "solved_tail": bell_draw(keys[5], (M, TAIL), 0.2, 1.2, ((1, 256),), jnp.float32),
    }


def multiply(left, right):
    return jnp.dot(left, right, precision=lax.Precision.HIGHEST, preferred_element_type=jnp.float32)


def reference(rhs_panel, diag_inverse, sub_block, lower_panels, rhs_tail, solved_tail):
    forward_left = multiply(rhs_panel[0], diag_inverse[0].T)
    reduced = rhs_panel[1] - multiply(forward_left, sub_block.T)
    forward_right = multiply(reduced, diag_inverse[1].T)
    joined = jnp.concatenate([forward_left, forward_right], axis=1)
    rhs_updated = rhs_tail - multiply(joined, lower_panels.T)
    summed = multiply(solved_tail, lower_panels)
    panel_width = diag_inverse.shape[1]
    solved_right = multiply(forward_right - summed[:, panel_width:], diag_inverse[1])
    residue = forward_left - multiply(solved_right, sub_block) - summed[:, :panel_width]
    solved_left = multiply(residue, diag_inverse[0])
    return rhs_updated, jnp.stack([solved_left, solved_right])
```

```python
import jax
import jax.numpy as jnp
from jax import lax
from jax.sharding import Mesh, PartitionSpec as P

HIGH = lax.Precision.HIGH
HIGHEST = lax.Precision.HIGHEST
SIZE = dict(zl=2, y=4, c=2, zh=4, x=4)
PROW = ("zl", "y", "c")
PCOL = ("zh", "x")


def dot(left, right, dims, precision):
    return lax.dot_general(
        left, right, (dims, ((), ())), precision=precision, preferred_element_type=jnp.float32
    )


def mm(left, right, precision=HIGHEST):
    return dot(left, right, ((1,), (0,)), precision)


def mm_t(left, right, precision=HIGHEST):
    return dot(left, right, ((1,), (1,)), precision)


def shift(v, axis, step):
    n = SIZE[axis]
    return lax.ppermute(v, axis, [(i, (i - step) % n) for i in range(n)])


def pick(stacked, index):
    return lax.dynamic_index_in_dim(stacked, index, 0, keepdims=False)


def gather_rel(v, axis):
    return [v] + [shift(v, axis, t) for t in range(1, SIZE[axis])]


def natural(blocks, axis):
    n = SIZE[axis]
    me = lax.axis_index(axis)
    stacked = jnp.stack(blocks + blocks[:-1])
    return lax.dynamic_slice_in_dim(stacked, (n - me) % n, n, 0)


def gather(v, axis):
    return natural(gather_rel(v, axis), axis)


def scatter_sum(piece, axis):
    n = SIZE[axis]
    me = lax.axis_index(axis)
    order = [2, 1, 3] if n == 4 else [1]
    got = [shift(piece(t, (me + t) % n), axis, -t) for t in order]
    total = piece(0, me)
    for g in got:
        total = total + g
    return total


def scatter_sum_of(stacked, axis):
    return scatter_sum(lambda t, at: pick(stacked, at), axis)


def spread_blocks(v, axes, n):
    return lax.all_to_all(jnp.broadcast_to(v[None], (n,) + v.shape), axes, 0, 0, tiled=True)


def sum_blocks(stacked, axes):
    return jnp.sum(lax.all_to_all(stacked, axes, 0, 0, tiled=True), axis=0)


def core_pair(v):
    other = shift(v, "c", 1)
    first = lax.axis_index("c") == 0
    return jnp.stack([jnp.where(first, v, other), jnp.where(first, other, v)])


def to_cols(blocks):
    n, r, w = blocks.shape
    return jnp.transpose(blocks, (1, 0, 2)).reshape(r, n * w)


def from_cols(v, n):
    r = v.shape[0]
    return jnp.transpose(v.reshape(r, n, v.shape[1] // n), (1, 0, 2))


def gather_prow(v):
    a = spread_blocks(v, ("zl", "y"), 8)
    return jnp.moveaxis(core_pair(a), 0, 1)


def after(v, done):
    return lax.optimization_barrier((v, done))[0]


def join(*arrays):
    return lax.optimization_barrier(arrays)


def roll_to_natural(v, axis_name, dim):
    n = SIZE[axis_name]
    me = lax.axis_index(axis_name)
    out = v
    for k in range(1, n):
        out = jnp.where(me == k, jnp.roll(v, k, dim), out)
    return out


def local(rhs_panel, diag_inverse, sub_block, lower_panels, rhs_tail, solved_tail):
    core = lax.axis_index("c")
    zl = lax.axis_index("zl")
    y = lax.axis_index("y")
    x = lax.axis_index("x")
    M = solved_tail.shape[0]
    half = M // 2
    W = lower_panels.shape[1] // 2
    T = W // 16
    R = M // 16
    S = 4 * T
    rows = lower_panels.shape[0]

    start = core * half + zl * (half // 2) + y * R
    b_rows = lax.dynamic_slice_in_dim(rhs_panel, start, R, 1)
    l10 = lax.all_gather(sub_block, PCOL).reshape(W, T)
    pairs = []
    for to in range(16):
        zh, xx = divmod(to, 4)
        for b in range(16):
            pairs.append(((xx * 4 + zh) * 16 + b, b * 16 + to))
    tiles = lax.ppermute(diag_inverse, PROW + PCOL, pairs)
    q2 = solved_tail.reshape(2, half, rows)
    q_own = pick(q2, core)
    q_sib = shift(pick(q2, 1 - core), "c", 1)
    p_own = lower_panels
    p_sib = shift(lower_panels, "c", 1)
    b_all = spread_blocks(b_rows, PCOL, 16)
    b_all, tiles, q_sib, p_sib = join(b_all, tiles, q_sib, p_sib)

    def piece1(t):
        at = W + ((x + t) % 4) * S
        own = lax.dynamic_slice_in_dim(p_own, at, S, 1)
        sib = lax.dynamic_slice_in_dim(p_sib, at, S, 1)
        return mm(q_own, own, HIGH) + mm(q_sib, sib, HIGH)

    def piece0(t):
        own = pick_rows(q_own, t)
        sib = pick_rows(q_sib, t)
        return mm(own, p_own[:, :W], HIGH) + mm(sib, p_sib[:, :W], HIGH)

    def pick_rows(v, t):
        v = v.reshape(2, 4, R, rows)
        return lax.dynamic_slice_in_dim(v, (y + t) % 4, 1, 1).reshape(2 * R, rows)

    s1 = {}
    s0 = {}
    for t in (2, 1, 3, 0):
        s1[t] = piece1(t)
        s0[t] = piece0(t)
    r1 = {t: shift(s1[t], "x", -t) for t in (2, 1, 3)}
    r0 = {t: shift(s0[t], "y", -t) for t in (2, 1, 3)}

    full = gather_prow(tiles).reshape(16, 2, T, T)
    full, s1[0], s0[0] = join(full, s1[0], s0[0])
    d0 = to_cols(full[:, 0])
    d1 = to_cols(full[:, 1])
    b0 = to_cols(b_all[:, 0])
    b1 = to_cols(b_all[:, 1])
    z0 = mm_t(b0, d0)
    bd = mm_t(b1, d1)
    z0_all = spread_blocks(z0, ("x", "zh"), 16)
    z0_all, r1[2], r0[2], d1 = join(z0_all, r1[2], r0[2], d1)
    z0_all = to_cols(z0_all)
    k = gather_prow(mm(d1, l10))
    k, r1[1], r0[1], z0_all = join(k, r1[1], r0[1], z0_all)
    k = to_cols(k.reshape(16, T, T))
    z1 = bd - mm_t(z0_all, k)
    q1 = spread_blocks(z1, "zh", 4)
    q1, r1[3], r0[3] = join(q1, r1[3], r0[3])
    q1 = to_cols(q1)
    q0 = lax.dynamic_slice_in_dim(z0_all, x * S, S, 1)

    g1 = s1[0] + r1[2] + r1[1] + r1[3]
    g0 = s0[0] + r0[2] + r0[1] + r0[3]
    g1 = jnp.transpose(g1.reshape(2, 4, R, S), (1, 0, 2, 3))
    g0 = jnp.transpose(g0.reshape(2, R, 4, S), (2, 0, 1, 3))
    g1 = scatter_sum_of(g1, "y")
    g0 = scatter_sum_of(g0, "x")
    v = gather(jnp.stack([q0, q1]), "zl")
    v, g1, g0 = join(v, g1, g0)
    g = jnp.stack([g0, g1], axis=1)
    g = jnp.transpose(g.reshape(2, 2, R, 4, T), (0, 3, 1, 2, 4)).reshape(8, 2, R, T)
    g = sum_blocks(g, ("zl", "zh"))

    pend = z1 - g[1]
    part0 = from_cols(mm(pend, k), 16).reshape(4, 4, R, T)
    part0 = jnp.transpose(part0, (1, 0, 2, 3)).reshape(16, R, T)
    part = jnp.stack([from_cols(mm(pend, d1), 16), part0], axis=1)
    part = sum_blocks(part, PCOL)
    v0 = jnp.stack(gather_rel(v[:, 0], "y"))
    v1 = jnp.stack(gather_rel(v[:, 1], "x"))
    part, v0, v1 = join(part, v0, v1)
    sol1 = part[0]
    residue = z0 - part[1] - g[0]
    sol0 = sum_blocks(from_cols(mm(residue, d0), 16), PCOL)
    w0 = gather_rel(v0, "x")
    w1 = gather_rel(v1, "y")
    sol0, w0[1], w0[2], w1[1], w1[2] = join(sol0, w0[1], w0[2], w1[1], w1[2])
    solved = gather_prow(jnp.stack([sol0, sol1]))
    solved, w0[3], w1[3] = join(solved, w0[3], w1[3])
    solved = jnp.transpose(solved, (2, 1, 0, 3, 4)).reshape(2, M, T)

    lhs = [w0[t].reshape(half, S) for t in range(4)]
    w1 = jnp.stack(w1)
    lhs += [w1[:, t].reshape(half, S) for t in range(4)]

    def product(panels):
        total = 0.0
        for n in range(8):
            at = (n // 4) * W + ((x + n) % 4) * S
            total = total + mm_t(lhs[n], lax.dynamic_slice_in_dim(panels, at, S, 1), HIGH)
        return total

    theirs = shift(product(p_sib), "c", 1)
    mine = product(p_own)
    both = jnp.where(core == 0, jnp.stack([mine, theirs]), jnp.stack([theirs, mine]))
    both = roll_to_natural(both.reshape(2, 4, 2, R, rows), "y", 1)
    both = jnp.transpose(both, (0, 2, 1, 3, 4))
    rhs_updated = rhs_tail - both.reshape(M, rows)
    return rhs_updated, solved


def solution(mesh):
    fine = Mesh(mesh.devices.reshape(2, 4, 2, 4, 4), ("zl", "y", "c", "zh", "x"))
    every = PROW + PCOL
    return jax.shard_map(
        local,
        mesh=fine,
        in_specs=(
            P(None, None, PCOL),
            P(None, PROW, PCOL),
            P(PCOL, PROW),
            P(every, None),
            P(None, every),
            P(None, every),
        ),
        out_specs=(P(None, every), P(None, None, PCOL)),
        check_vma=False,
    )
```
